32 devices in a mesh: grid: 4 (over z), rep: 8 (over y, x, core).
Axes of the slice: x: 2, y: 2, z: 4, core: 2. Of those that a mesh axis runs over, the one named last changes fastest.
Arguments:
- amplitudes: bfloat16 [96, 960, 960], P('grid', 'rep'), may hold values from -6 to 6
- vvvv_panel: bfloat16 [960, 960, 1920], P('rep', 'grid'), may hold values from -0.01171875 to 0.01171875
- fock_window: bfloat16 [960, 2], P('rep'), may hold values from -0.375 to 0.375
- orbital_irrep: int32 [960], replicated, may hold values from 0 to 3, as said below
- pair_irrep: int32 [96], replicated, may hold values from 0 to 3
- virtual_panel: int32 [2], replicated, may hold values from 0 to 959
Outputs:
- residual: float32 [96, 2, 960], P('rep', None, 'grid')
The draws below stay inside these ranges and needn't reach their ends.
Inputs may be any that keep to these rules, and one draw needn't show every extreme that they name: `orbital_irrep`: the virtual orbitals form four contiguous runs of 240 orbitals each; every orbital of a run has the same irrep, and each irrep 0 to 3 holds exactly one run, in an order that varies from draw to draw.
All inputs are finite; a program needn't handle non-finite values.
Results may differ from the reference program's by a relative error of at most 0.00035.
Values may be sent and summed in bfloat16 or wider, within the bound.
A program may use at most 384 MiB of HBM per device.

```python
import jax
import jax.numpy as jnp
from jax import lax

V = 960
PAIRS = 96
B_WIN = 2


def draw_orbital_irrep(key, part):
    key = jax.random.fold_in(key, 11)
    order = jax.random.permutation(key, 4).astype(jnp.int32)
    return jnp.repeat(order, V // 4, total_repeat_length=V).astype(jnp.int32)


def set_ends(result, rng, low, high):
    spot = [jax.random.randint(jax.random.fold_in(rng, axis), (), 0, length) for axis, length in enumerate(result.shape)]
    main_axis = result.shape.index(max(result.shape))
    beside = spot[:main_axis] + [(spot[main_axis] + 1) % result.shape[main_axis]] + spot[main_axis + 1:]
    return result.at[tuple(spot)].set(low).at[tuple(beside)].set(high)


def level_of(stream_key, extent, cuts, least, largest):
    def one(dim, shards_of):
        draws = jax.random.uniform(jax.random.fold_in(jax.random.fold_in(stream_key, 6), dim), (shards_of,), jnp.float32, least / len(cuts), largest / len(cuts))
        return jnp.repeat(jnp.exp(draws), extent[dim] // shards_of).reshape((-1,) + (1,) * (len(extent) - dim - 1))

    loudness = one(*cuts[0])
    for cut in cuts[1:]:
        loudness = loudness * one(*cut)
    return loudness


def centred(stream_key, shape, spread, bound, split=(), held_as=jnp.bfloat16):
    loudness = level_of(stream_key, shape, split, -0.22, 0.18) if split else 1.0
    result = jax.random.normal(stream_key, shape, jnp.float32) * spread * loudness
    return jnp.minimum(jnp.maximum(result, -bound), bound).astype(held_as)


def setup_inputs(seed: int = 0) -> dict:
    splits = jax.random.split(jax.random.key(seed), 7)
    return {
        "amplitudes": centred(splits[0], (PAIRS, V, V), 1.0, 6.0, ((0, 4), (1, 8))),
        "vvvv_panel": centred(splits[1], (V, V, B_WIN * V), (V * V // 4) ** -0.5, 0.01171875, ((0, 8), (1, 4))),
        "fock_window": centred(splits[2], (V, B_WIN), (V // 4) ** -0.5, 0.375, ((0, 8),)),
        "orbital_irrep": draw_orbital_irrep(jax.random.fold_in(splits[6], 71), 0),
        "pair_irrep": set_ends(jax.random.randint(splits[4], (PAIRS,), 0, 4), jax.random.fold_in(splits[4], 1), 0, 3).astype(jnp.int32),
        "virtual_panel": jax.random.randint(splits[5], (B_WIN,), 0, V).astype(jnp.int32),
    }


def reference(amplitudes, vvvv_panel, fock_window, orbital_irrep, pair_irrep, virtual_panel):
    panel_irrep = orbital_irrep[virtual_panel]
    pair_sym = jnp.bitwise_xor(orbital_irrep[:, None], orbital_irrep[None, :])
    amp_mask = pair_sym[None, :, :] == pair_irrep[:, None, None]
    masked_amps = jnp.where(amp_mask, amplitudes, jnp.zeros_like(amplitudes))
    target_sym = jnp.bitwise_xor(panel_irrep[:, None], orbital_irrep[None, :])
    target_cols = jnp.transpose(target_sym)
    fock_mask = orbital_irrep[:, None] == panel_irrep[None, :]
    masked_f = jnp.where(fock_mask, fock_window, jnp.zeros_like(fock_window))

    def ladder_step(total, virt_index):
        w_slice = lax.dynamic_index_in_dim(vvvv_panel, virt_index, 0, keepdims=False)
        w_slice = w_slice.reshape(V, B_WIN, V)
        sym_row = lax.dynamic_index_in_dim(pair_sym, virt_index, 0, keepdims=False)
        w_mask = sym_row[None, None, :] == target_cols[:, :, None]
        w_masked = jnp.where(w_mask, w_slice, jnp.zeros_like(w_slice))
        amp_slice = lax.dynamic_index_in_dim(masked_amps, virt_index, 1, keepdims=False)
        term = jnp.einsum("pd,abd->pba", amp_slice.astype(jnp.float32), w_masked.astype(jnp.float32))
        return total + term, None

    start_total = jnp.zeros((PAIRS, B_WIN, V), jnp.float32)
    ladder, _ = lax.scan(ladder_step, start_total, jnp.arange(V, dtype=jnp.int32))
    fock_term = jnp.einsum("pca,cb->pba", masked_amps.astype(jnp.float32), masked_f.astype(jnp.float32))
    return ladder + fock_term
```

```python
import functools

import jax
import jax.numpy as jnp
from jax import lax
from jax.experimental import pallas as pl
from jax.experimental.pallas import tpu as pltpu
from jax.sharding import PartitionSpec as P

LANES = 128
SPAN = 256
CHUNKS = 3


def ladder_kernel(steps, panel, scalars, fock, amps, *refs):
    tiles = refs[: 3 * panel]
    out = refs[3 * panel]
    acc, facc, wide, turned = refs[3 * panel + 1 :]
    step = pl.program_id(0)
    depth, cols, _ = tiles[0].shape

    @pl.when(step == 0)
    def _():
        acc[...] = jnp.zeros_like(acc)
        facc[...] = jnp.zeros_like(facc)

    lane = lax.broadcasted_iota(jnp.int32, (cols, LANES), 1)
    for c in range(depth):
        at = slice(c * SPAN, (c + 1) * SPAN)
        part = amps[:, at].astype(jnp.float32)
        for b in range(panel):
            facc[b] += fock[(step * depth + c) * panel + b] * part
            turned[b, :, at] = pltpu.roll(part, scalars[panel + b], 1).astype(jnp.bfloat16)
            first, second, third = tiles[3 * b : 3 * b + 3]
            low = jnp.where(lane >= scalars[2 * panel + b], first[c], third[c])
            wide[b, :, c * SPAN : c * SPAN + LANES] = low
            wide[b, :, c * SPAN + LANES : (c + 1) * SPAN] = second[c]
    for b in range(panel):
        acc[b] += lax.dot_general(turned[b], wide[b], (((1,), (1,)), ((), ())), preferred_element_type=jnp.float32)

    @pl.when(step == steps - 1)
    def _():
        for b in range(panel):
            own = pltpu.roll(facc[b], scalars[3 * panel], 1)
            out[b] = acc[b] + own[:, :cols]


def ladder(scalars, fock, amps, w, first_row, rows, full_virt):
    panel = w.shape[2] // full_virt
    cols = w.shape[1]
    pairs = amps.shape[0]
    depth = max(d for d in range(1, 9) if rows % d == 0)
    steps = rows // depth
    last_tile = w.shape[2] // LANES - 1
    offset = first_row // depth

    def tile_map(b, j):
        def index(i, scalars, fock):
            return (i + offset, 0, jnp.minimum(scalars[b] + j, last_tile))

        return index

    w_specs = [pl.BlockSpec((depth, cols, LANES), tile_map(b, j)) for b in range(panel) for j in range(3)]
    return pl.pallas_call(
        functools.partial(ladder_kernel, steps, panel),
        out_shape=jax.ShapeDtypeStruct((panel, pairs, cols), jnp.float32),
        grid_spec=pltpu.PrefetchScalarGridSpec(
            num_scalar_prefetch=2,
            grid=(steps,),
            in_specs=[pl.BlockSpec((pairs, depth * SPAN), lambda i, s, f: (0, i))] + w_specs,
            out_specs=pl.BlockSpec((panel, pairs, cols), lambda i, s, f: (0, 0, 0)),
            scratch_shapes=[
                pltpu.VMEM((panel, pairs, cols), jnp.float32),
                pltpu.VMEM((panel, pairs, SPAN), jnp.float32),
                pltpu.VMEM((panel, cols, depth * SPAN), jnp.bfloat16),
                pltpu.VMEM((panel, pairs, depth * SPAN), jnp.bfloat16),
            ],
        ),
        compiler_params=pltpu.CompilerParams(vmem_limit_bytes=40 * 1024 * 1024),
        cost_estimate=pl.CostEstimate(
            flops=2 * pairs * rows * SPAN * cols * panel,
            bytes_accessed=rows * cols * 3 * LANES * panel * 2 + pairs * rows * SPAN * 2,
            transcendentals=0,
        ),
    )(scalars, fock, amps, *([w] * (3 * panel)))


def shards(amplitudes, vvvv_panel, fock_window, orbital_irrep, pair_irrep, virtual_panel):
    pair_local, virt_local, full_virt = amplitudes.shape
    col_local = vvvv_panel.shape[1]
    panel = vvvv_panel.shape[2] // full_virt
    run = full_virt // 4
    grid_index = lax.axis_index("grid")
    rep_index = lax.axis_index("rep")
    col_start = grid_index * col_local

    run_irreps = orbital_irrep[::run]
    places = jnp.sum(jnp.where(run_irreps[None, :] == jnp.arange(4)[:, None], jnp.arange(4)[None, :], 0), axis=1).astype(jnp.int32)
    c_irrep = run_irreps[rep_index * virt_local // run]
    a_irrep = run_irreps[col_start // run]
    panel_irrep = orbital_irrep[virtual_panel]

    own_pairs = lax.dynamic_slice_in_dim(pair_irrep, grid_index * pair_local, pair_local, 0)
    pair_run = places[own_pairs ^ c_irrep]
    span_count = -(-full_virt // SPAN)
    compact = jnp.zeros((pair_local, virt_local, SPAN), amplitudes.dtype)
    for q in range(span_count):
        width = min(SPAN, full_virt - q * SPAN)
        piece = amplitudes[:, :, q * SPAN : q * SPAN + width]
        piece = jnp.pad(piece, ((0, 0), (0, 0), (0, SPAN - width)))
        lane_run = (q * SPAN + jnp.arange(SPAN, dtype=jnp.int32)) // run
        compact = jnp.where(lane_run[None, None, :] == pair_run[:, None, None], piece, compact)

    panel_run = places[c_irrep ^ a_irrep ^ panel_irrep]
    starts = jnp.arange(panel, dtype=jnp.int32) * full_virt
    first = starts + panel_run * run
    first_tile = first // LANES
    shift = (starts - first_tile * LANES) % SPAN
    skip = first - first_tile * LANES
    own_shift = (-col_start) % SPAN
    scalars = jnp.concatenate([first_tile, shift, skip, own_shift[None]]).astype(jnp.int32)
    masked_f = jnp.where(panel_irrep[None, :] == c_irrep, fock_window, jnp.zeros_like(fock_window)).astype(jnp.float32)

    chunks = CHUNKS if virt_local % CHUNKS == 0 else 1
    rows = virt_local // chunks
    total = None
    for k in range(chunks):
        part = compact[:, k * rows : (k + 1) * rows, :].reshape(pair_local, rows * SPAN)
        gathered = lax.all_gather(part, "grid", axis=0, tiled=True)
        fock = masked_f[k * rows : (k + 1) * rows].reshape(-1)
        term = ladder(scalars, fock, gathered, vvvv_panel, k * rows, rows, full_virt)
        total = term if total is None else total + term

    pair_count = total.shape[1]
    keep = pair_irrep[None, :] == (panel_irrep ^ a_irrep)[:, None]
    partials = jnp.where(keep[:, :, None], total, 0.0)
    partials = jnp.swapaxes(partials, 0, 1).reshape(pair_count, panel * col_local)
    summed = lax.psum_scatter(partials, "rep", scatter_dimension=0, tiled=True)
    return summed.reshape(pair_count // lax.axis_size("rep"), panel, col_local)


def solution(mesh):
    return jax.shard_map(
        shards,
        mesh=mesh,
        in_specs=(P("grid", "rep", None), P("rep", "grid", None), P("rep", None), P(), P(), P()),
        out_specs=P("rep", None, "grid"),
        check_vma=False,
    )
```

```python
import functools

import jax
import jax.numpy as jnp
from jax import lax
from jax.experimental import pallas as pl
from jax.experimental.pallas import tpu as pltpu
from jax.sharding import PartitionSpec as P

LANES = 128
SPAN = 256
MESH = pl.DeviceIdType.MESH


def ladder_kernel(
    n, reps, full_virt, own, fock, orbital, panel_irreps, pair_irreps, w, out,
    amps, even, odd, acc, facc, wide, turned, terms, landed, send_sem, recv_sem, w_sem, term_send, term_recv,
):
    me = lax.axis_index("grid")
    rep = lax.axis_index("rep")
    chunks, pair_local, _ = own.shape
    depth, cols, width = even.shape
    panel = acc.shape[0]
    run = full_virt // 4
    rows = chunks * depth
    has_right, has_left = me < n - 1, me > 0
    right, left = jnp.minimum(me + 1, n - 1), jnp.maximum(me - 1, 0)

    def w_copy(chunk, slot):
        return pltpu.make_async_copy(w.at[pl.ds(chunk * depth, depth)], (even, odd)[slot], w_sem.at[slot])

    w_copy(0, 0).start()
    w_copy(1, 1).start()

    barrier = pltpu.get_barrier_semaphore()
    for there, other in ((has_right, right), (has_left, left)):
        @pl.when(there)
        def _():
            pl.semaphore_signal(barrier, inc=1, device_id={"grid": other}, device_id_type=MESH)
    for d in range(1, reps):
        pl.semaphore_signal(barrier, inc=1, device_id={"rep": lax.rem(rep + d, reps)}, device_id_type=MESH)
    pl.semaphore_wait(barrier, reps - 1 + jnp.minimum(me, 1) + jnp.minimum(n - 1 - me, 1))

    def copy(owner, chunk, way):
        return pltpu.make_async_remote_copy(
            src_ref=amps.at[owner, chunk],
            dst_ref=amps.at[owner, chunk],
            send_sem=send_sem.at[way, owner, chunk],
            recv_sem=recv_sem.at[owner, chunk],
            device_id={"grid": (right, left)[way]},
            device_id_type=MESH,
        )

    def pass_on(i):
        @pl.when(i < chunks)
        def _():
            amps[me, i] = own[i]

            @pl.when(has_right)
            def _():
                copy(me, i, 0).start()

            @pl.when(has_left)
            def _():
                copy(me, i, 1).start()

        for s in range(1, n):
            chunk = i - s
            valid = jnp.logical_and(chunk >= 0, chunk < chunks)

            @pl.when(jnp.logical_and(valid, me >= s))
            def _():
                copy(me - s, chunk, 0).wait_recv()

                @pl.when(has_right)
                def _():
                    copy(me - s, chunk, 0).start()

            @pl.when(jnp.logical_and(valid, me + s < n))
            def _():
                copy(me + s, chunk, 1).wait_recv()

                @pl.when(has_left)
                def _():
                    copy(me + s, chunk, 1).start()

    c_irrep = orbital[rep * rows]
    a_irrep = orbital[me * cols]
    panel_irrep = [panel_irreps[b] for b in range(panel)]
    starts = []
    for b in range(panel):
        wanted = c_irrep ^ a_irrep ^ panel_irrep[b]
        place = jnp.int32(0)
        for r in range(1, 4):
            place = place + jnp.where(orbital[r * run] == wanted, r, 0)
        starts.append(b * full_virt + place * run)

    acc[...] = jnp.zeros_like(acc)
    facc[...] = jnp.zeros_like(facc)
    lane = lax.broadcasted_iota(jnp.int32, (cols, LANES), 1)

    def multiply(chunk, slot):
        held = (even, odd)[slot]
        w_copy(chunk, slot).wait()
        for c in range(depth):
            at = slice(c * SPAN, (c + 1) * SPAN)
            part = jnp.concatenate([amps[s, chunk, :, at].astype(jnp.float32) for s in range(n)], axis=0)
            for b in range(panel):
                facc[b] += fock[(chunk * depth + c) * panel + b] * part
                near = pltpu.roll(part, b * full_virt % SPAN, 1) if b * full_virt % SPAN else part
                turned[b, :, at] = near.astype(jnp.bfloat16)
                for half in range(2):
                    picked = None
                    for t in range(b * full_virt // LANES, -(-(b + 1) * full_virt // LANES)):
                        if t % 2 != half:
                            continue
                        here = held[c, :, t * LANES : (t + 1) * LANES]
                        inside = jnp.logical_and(lane >= starts[b] - t * LANES, lane < starts[b] + run - t * LANES)
                        picked = here if picked is None else jnp.where(inside, here, picked)
                    wide[b, :, c * SPAN + half * LANES : c * SPAN + (half + 1) * LANES] = picked
        for b in range(panel):
            acc[b] += lax.dot_general(turned[b], wide[b], (((1,), (1,)), ((), ())), preferred_element_type=jnp.float32)

        @pl.when(chunk + 2 < chunks)
        def _():
            w_copy(chunk + 2, slot).start()

    @pl.loop(0, n - 1)
    def _(i):
        pass_on(i)

    @pl.loop(0, chunks // 2)
    def _(pair):
        for slot in range(2):
            chunk = pair * 2 + slot
            pass_on(chunk + n - 1)
            multiply(chunk, slot)

    own_shift = (n * cols * SPAN - me * cols) % SPAN
    out_rows = out.shape[1]
    for b in range(panel):
        own_cols = pltpu.roll(facc[b], own_shift, 1)[:, :cols]
        whole = acc[b] + own_cols * (panel_irrep[b] == c_irrep).astype(jnp.float32)
        whole = jnp.where(pair_irreps[...] == (panel_irrep[b] ^ a_irrep), whole, 0.0)
        for r in range(reps):
            terms[r, b] = whole[r * out_rows : (r + 1) * out_rows]

    def term_copy(d):
        peer = lax.rem(rep + d, reps)
        return pltpu.make_async_remote_copy(
            src_ref=terms.at[peer],
            dst_ref=landed.at[d],
            send_sem=term_send.at[d],
            recv_sem=term_recv.at[d],
            device_id={"rep": peer},
            device_id_type=MESH,
        )

    for d in range(1, reps):
        term_copy(d).start()
    total = terms[rep]
    for d in range(1, reps):
        term_copy(d).wait_recv()
        total = total + landed[d]
    out[...] = total
    for d in range(1, reps):
        term_copy(d).wait_send()

    @pl.loop(0, chunks)
    def _(chunk):
        for owner in range(n):
            @pl.when(jnp.logical_and(has_right, owner <= me))
            def _():
                copy(owner, chunk, 0).wait_send()

            @pl.when(jnp.logical_and(has_left, owner >= me))
            def _():
                copy(owner, chunk, 1).wait_send()


def ladder(own, fock, orbital, panel_irreps, pair_irreps, w, n, reps, full_virt):
    panel = w.shape[2] // full_virt
    rows, cols, width = w.shape
    chunks, pair_local, span = own.shape
    depth = rows // chunks
    pairs = n * pair_local
    smem = pl.BlockSpec(memory_space=pltpu.SMEM)
    vmem = pl.BlockSpec(memory_space=pltpu.VMEM)
    return pl.pallas_call(
        functools.partial(ladder_kernel, n, reps, full_virt),
        out_shape=jax.ShapeDtypeStruct((panel, pairs // reps, cols), jnp.float32),
        in_specs=[vmem, smem, smem, smem, vmem, pl.BlockSpec(memory_space=pl.ANY)],
        out_specs=vmem,
        scratch_shapes=[
            pltpu.VMEM((n, chunks, pair_local, span), jnp.bfloat16),
            pltpu.VMEM((depth, cols, width), jnp.bfloat16),
            pltpu.VMEM((depth, cols, width), jnp.bfloat16),
            pltpu.VMEM((panel, pairs, cols), jnp.float32),
            pltpu.VMEM((panel, pairs, SPAN), jnp.float32),
            pltpu.VMEM((panel, cols, span), jnp.bfloat16),
            pltpu.VMEM((panel, pairs, span), jnp.bfloat16),
            pltpu.VMEM((reps, panel, pairs // reps, cols), jnp.float32),
            pltpu.VMEM((reps, panel, pairs // reps, cols), jnp.float32),
            pltpu.SemaphoreType.DMA((2, n, chunks)),
            pltpu.SemaphoreType.DMA((n, chunks)),
            pltpu.SemaphoreType.DMA((2,)),
            pltpu.SemaphoreType.DMA((reps,)),
            pltpu.SemaphoreType.DMA((reps,)),
        ],
        compiler_params=pltpu.CompilerParams(vmem_limit_bytes=44 * 1024 * 1024, collective_id=0, has_side_effects=True),
        cost_estimate=pl.CostEstimate(
            flops=2 * pairs * rows * SPAN * cols * panel, bytes_accessed=rows * cols * width * 2, transcendentals=0
        ),
    )(own, fock, orbital, panel_irreps, pair_irreps, w)


def pick(table, index):
    found = jnp.zeros_like(index)
    for r in range(4):
        found = jnp.where(index == r, table[r], found)
    return found


def shards(amplitudes, vvvv_panel, fock_window, orbital_irrep, pair_irrep, virtual_panel):
    pair_local, virt_local, full_virt = amplitudes.shape
    run = full_virt // 4
    grid_index = lax.axis_index("grid")
    rep_index = lax.axis_index("rep")

    runs = [orbital_irrep[r * run] for r in range(4)]
    c_irrep = pick(runs, rep_index * virt_local // run)

    own_pairs = lax.dynamic_slice_in_dim(pair_irrep, grid_index * pair_local, pair_local, 0)
    wanted = own_pairs ^ c_irrep
    pair_run = sum(jnp.where(runs[r] == wanted, r, 0) for r in range(1, 4))
    span_count = -(-full_virt // SPAN)
    compact = jnp.zeros((pair_local, virt_local, SPAN), amplitudes.dtype)
    for q in range(span_count):
        width = min(SPAN, full_virt - q * SPAN)
        piece = amplitudes[:, :, q * SPAN : q * SPAN + width]
        piece = jnp.pad(piece, ((0, 0), (0, 0), (0, SPAN - width)))
        lane_run = (q * SPAN + jnp.arange(SPAN, dtype=jnp.int32)) // run
        compact = jnp.where(lane_run[None, None, :] == pair_run[:, None, None], piece, compact)

    depth = max(d for d in range(1, 9) if virt_local % (2 * d) == 0)
    chunks = virt_local // depth
    own = jnp.swapaxes(compact.reshape(pair_local, chunks, depth * SPAN), 0, 1)
    fock = fock_window.astype(jnp.float32).reshape(-1)
    sizes = lax.axis_size("grid"), lax.axis_size("rep")
    summed = ladder(own, fock, orbital_irrep, pick(runs, virtual_panel // run), pair_irrep[:, None], vvvv_panel, *sizes, full_virt)
    return jnp.swapaxes(summed, 0, 1)


def solution(mesh):
    return jax.shard_map(
        shards,
        mesh=mesh,
        in_specs=(P("grid", "rep", None), P("rep", "grid", None), P("rep", None), P(), P(), P()),
        out_specs=P("rep", None, "grid"),
        check_vma=False,
    )
```
